32 devices in a mesh: seq: 8 (over z, y), head: 4 (over x, core).
Axes of the slice: x: 2, y: 2, z: 4, core: 2. Of those that a mesh axis runs over, the one named last changes fastest.
Arguments:
- x_raw: bfloat16 [2048, 4096], P('seq', 'head'), may hold values from -6 to 6
- bc_raw: bfloat16 [2048, 256], P('seq'), may hold values from -6 to 6
- gate_z: bfloat16 [2048, 4096], P('seq', 'head'), may hold values from -6 to 6
- step_size: float32 [2048, 64], P('seq', 'head'), may hold values from 0.002 to 0.05
- log_decay: float32 [2048, 64], P('seq', 'head'), may hold values from -1 to 0, as said below
- doc_ids: int32 [2048], P('seq'), may hold values from 0 to 3, as said below
- conv_x: float32 [4, 4096], P(None, 'head'), may hold values from -3 to 3
- conv_bc: float32 [4, 256], replicated, may hold values from -3 to 3
- skip: float32 [64], P('head'), may hold values from 0.5 to 2
- norm_gain: float32 [4096], P('head'), may hold values from 0.25 to 1.75
Outputs:
- mixed: bfloat16 [2048, 4096], P('seq', 'head')
The draws below stay inside these ranges and needn't reach their ends.
Inputs may be any that keep to these rules, and one draw needn't show every extreme that they name: `doc_ids`: document ids never fall along the sequence; each document has 1 to 1024 tokens, one exactly 1024. `log_decay`: every entry is negative.
All inputs are finite; a program needn't handle non-finite values.
Results may differ from the reference program's by a relative error of at most 0.005.
Values may be sent and summed in bfloat16 or wider, within the bound.
A program may use at most 192 MiB of HBM per device.

```python
import jax
import jax.numpy as jnp
from jax import lax

H = 64
P_SIZE = 64
N = 128
GROUP = 256
KW = 4
TOK_DEV = 256
JOINED_ITEMS = 2048
MAX_TEXT_SPAN = 1024
DOCS = 4


def text_layout(key):
    sampler_seeds = jax.random.split(jax.random.fold_in(key, 29), 3)
    remaining = JOINED_ITEMS - MAX_TEXT_SPAN
    pieces = DOCS - 1
    weights = jax.random.randint(sampler_seeds[0], (pieces,), 1, 4).astype(jnp.int32)
    running = jnp.cumsum(weights).astype(jnp.int32)
    boundaries = (remaining * running[:-1] // running[-1]).astype(jnp.int32)
    first_dev = jax.random.randint(sampler_seeds[1], (), 0, remaining // TOK_DEV).astype(jnp.int32)
    offset = jax.random.randint(sampler_seeds[2], (), TOK_DEV // 4, 3 * TOK_DEV // 4 + 1).astype(jnp.int32)
    doc_start = first_dev * TOK_DEV + offset
    nearest = jnp.argmin(jnp.abs(boundaries - doc_start))
    placed = jnp.where(jnp.arange(pieces - 1) == nearest, doc_start, boundaries)
    placed = jnp.sort(placed).astype(jnp.int32)
    return (doc_start, placed)


def draw_doc_ids(key, part):
    doc_start, placed = text_layout(key)
    positions = jnp.arange(JOINED_ITEMS, dtype=jnp.int32)
    line_index = jnp.where(positions < doc_start, positions, positions - MAX_TEXT_SPAN)
    counted = jnp.sum((placed[None, :] <= line_index[:, None]).astype(jnp.int32), axis=1)
    inside = (positions >= doc_start) & (positions < doc_start + MAX_TEXT_SPAN)
    after_long = (positions >= doc_start + MAX_TEXT_SPAN).astype(jnp.int32)
    long_id = jnp.sum((placed < doc_start).astype(jnp.int32)) + 1
    return jnp.where(inside, long_id, counted + after_long).astype(jnp.int32)


def draw_step_size(key, part):
    doc_start, placed = text_layout(key)
    sampler_seeds = jax.random.split(jax.random.fold_in(key, 13), 3)
    spread_rate = jnp.exp(jax.random.uniform(sampler_seeds[0], (JOINED_ITEMS, H), jnp.float32, jnp.log(0.00505), jnp.log(0.0495)))
    early_rate = jax.random.uniform(sampler_seeds[1], (JOINED_ITEMS, H), jnp.float32, 0.04, 0.05)
    late_rate = jax.random.uniform(sampler_seeds[2], (JOINED_ITEMS, H), jnp.float32, 0.002, 0.003)
    relative = jnp.arange(JOINED_ITEMS, dtype=jnp.int32) - doc_start
    early = (relative >= 0) & (relative < MAX_TEXT_SPAN // 8)
    later = (relative >= MAX_TEXT_SPAN // 8) & (relative < MAX_TEXT_SPAN)
    return jnp.where(early[:, None], early_rate, jnp.where(later[:, None], late_rate, spread_rate))


def draw_x_raw(key, part):
    doc_start, placed = text_layout(key)
    sampler_seeds = jax.random.split(jax.random.fold_in(key, 17), 1)
    values = jnp.clip(jax.random.normal(sampler_seeds[0], (JOINED_ITEMS, H * P_SIZE), jnp.float32), -6.0, 6.0)
    relative = jnp.arange(JOINED_ITEMS, dtype=jnp.int32) - doc_start
    quiet = (relative >= MAX_TEXT_SPAN - 3 * MAX_TEXT_SPAN // 16) & (relative < MAX_TEXT_SPAN)
    return (values * jnp.where(quiet, 0.05, 1.0)[:, None]).astype(jnp.bfloat16)


def draw_log_decay(key, part):
    sampler_seeds = jax.random.split(jax.random.fold_in(key, 11), 6)
    fast_share = 0.5
    fast_heads = jax.random.bernoulli(sampler_seeds[0], fast_share, (H,))
    slow_rate = jnp.exp(jax.random.uniform(sampler_seeds[1], (H,), jnp.float32, jnp.log(0.02), jnp.log(0.3))) / MAX_TEXT_SPAN
    fast_rate = jax.random.uniform(sampler_seeds[2], (H,), jnp.float32, 1.0 / 50.0, 1.0 / 30.0)
    forgetting_speed = jnp.where(fast_heads, fast_rate, slow_rate)
    multiplier_amplitude = jax.random.uniform(sampler_seeds[3], (JOINED_ITEMS, H), jnp.float32, 0.5, 2.0)
    contiguous_run_size = jax.random.bernoulli(sampler_seeds[4], 2.0 / MAX_TEXT_SPAN, (JOINED_ITEMS, 1)).astype(jnp.float32)
    stacked_level_index = jax.random.uniform(sampler_seeds[5], (JOINED_ITEMS, 1), jnp.float32, 0.2, 0.7)
    return -(forgetting_speed[None, :] * multiplier_amplitude) - contiguous_run_size * stacked_level_index


def steps_of(stream_key, dims, cuts, low, top_value):
    factor_of = 1.0
    for axis_at, blocks in cuts:
        heights = jax.random.uniform(jax.random.fold_in(jax.random.fold_in(stream_key, 6), axis_at), (blocks,), jnp.float32, low / len(cuts), top_value / len(cuts))
        factor_of = factor_of * jnp.repeat(jnp.exp(heights), dims[axis_at] // blocks).reshape((-1,) + (1,) * (len(dims) - 1 - axis_at))
    return factor_of


def normal_values(key, shape, spread, bound, cuts=(), kind=jnp.bfloat16):
    values = jax.random.normal(key, shape, jnp.float32) * spread
    if len(cuts) > 0:
        values = steps_of(key, shape, cuts, -0.22, 0.18) * values
    return jnp.clip(values, min=-bound, max=bound).astype(kind)


def setup_inputs(seed: int = 0) -> dict:
    seeds = jax.random.split(jax.random.key(seed), 11)
    x_raw = draw_x_raw(jax.random.fold_in(seeds[10], 71), 0)
    bc_raw = normal_values(seeds[1], (JOINED_ITEMS, 2 * N), 1.0, 6.0, ((0, 8),))
    gate_z = normal_values(seeds[2], (JOINED_ITEMS, H * P_SIZE), 1.0, 6.0, ((0, 8), (1, 4)))
    step_size = draw_step_size(jax.random.fold_in(seeds[10], 71), 0)
    log_decay = draw_log_decay(jax.random.fold_in(seeds[10], 71), 0)
    doc_ids = draw_doc_ids(jax.random.fold_in(seeds[10], 71), 0)
    conv_x = normal_values(seeds[6], (KW, H * P_SIZE), KW ** -0.5, 3.0, ((1, 4),), jnp.float32)
    conv_bc = normal_values(seeds[7], (KW, 2 * N), KW ** -0.5, 3.0, (), jnp.float32)
    skip = jnp.clip(0.5 + 1.5 * jax.random.uniform(seeds[8], (H,), jnp.float32) ** steps_of(seeds[8], (H,), ((0, 4),), -0.2, 0.2), 0.5, 2.0)
    norm_gain = jnp.clip(1.0 + 0.15 * jax.random.normal(seeds[9], (H * P_SIZE,), jnp.float32), 0.25, 1.75)
    return dict(x_raw=x_raw, bc_raw=bc_raw, gate_z=gate_z, step_size=step_size, log_decay=log_decay, doc_ids=doc_ids, conv_x=conv_x, conv_bc=conv_bc, skip=skip, norm_gain=norm_gain)


EPS = 1e-05

def conv_silu(raw, weight, doc_ids):
    rows = raw.shape[0]
    values = raw.astype(jnp.float32)
    total = jnp.zeros(raw.shape, jnp.float32)
    for k in range(KW):
        moved = jnp.concatenate([jnp.zeros((k, raw.shape[1]), jnp.float32), values[:rows - k]], axis=0)
        earlier = jnp.concatenate([jnp.full((k,), -1, jnp.int32), doc_ids[:rows - k]], axis=0)
        keep = (earlier == doc_ids).astype(jnp.float32)
        total = total + weight[k][None, :] * moved * keep[:, None]
    return lax.optimization_barrier(jax.nn.silu(total).astype(jnp.bfloat16))

def reference(x_raw, bc_raw, gate_z, step_size, log_decay, doc_ids, conv_x, conv_bc, skip, norm_gain):
    xconv = conv_silu(x_raw, conv_x, doc_ids)
    bconv = conv_silu(bc_raw, conv_bc, doc_ids)
    blocks = JOINED_ITEMS // GROUP
    xdt = (xconv.astype(jnp.float32).reshape(JOINED_ITEMS, H, P_SIZE) * step_size[:, :, None]).astype(jnp.bfloat16)
    xdt = lax.optimization_barrier(xdt)
    pieces = (xconv.reshape(blocks, GROUP, H, P_SIZE), xdt.reshape(blocks, GROUP, H, P_SIZE), bconv[:, :N].reshape(blocks, GROUP, N), bconv[:, N:].reshape(blocks, GROUP, N), gate_z.reshape(blocks, GROUP, H * P_SIZE), log_decay.reshape(blocks, GROUP, H), doc_ids.reshape(blocks, GROUP))
    lower = jnp.arange(GROUP)[:, None] >= jnp.arange(GROUP)[None, :]

    def block_step(carry, piece):
        state, prev_id = carry
        xs, xin, bmat, cmat, zs, decay, ids = piece
        cum = jnp.cumsum(decay, axis=0)
        gram = jnp.dot(cmat, bmat.T, preferred_element_type=jnp.float32)
        mask = ((ids[:, None] == ids[None, :]) & lower)[None]
        diff = cum.T[:, :, None] - cum.T[:, None, :]
        weights = jnp.where(mask, jnp.exp(jnp.where(mask, diff, 0.0)), 0.0) * gram[None]
        weights = lax.optimization_barrier(weights.astype(jnp.bfloat16))
        inner = jnp.einsum('hts,shp->thp', weights.astype(jnp.float32), xin.astype(jnp.float32))
        cont = (ids == prev_id).astype(jnp.float32)
        entry = jnp.exp(cum) * cont[:, None]
        entered = lax.optimization_barrier(state.astype(jnp.bfloat16))
        carried = jnp.einsum('tn,hpn->thp', cmat.astype(jnp.float32), entered.astype(jnp.float32)) * entry[:, :, None]
        scanned = inner + carried + skip[None, :, None] * xs.astype(jnp.float32)
        gated = scanned.reshape(GROUP, H * P_SIZE) * jax.nn.silu(zs.astype(jnp.float32))
        scale = lax.rsqrt(lax.optimization_barrier(jnp.sum(gated * gated, axis=1)) / (H * P_SIZE) + EPS)
        result = (gated * scale[:, None] * norm_gain[None, :]).astype(jnp.bfloat16)
        ends = jnp.where((ids == ids[-1])[:, None], jnp.exp(cum[-1][None, :] - cum), 0.0)
        written = lax.optimization_barrier((xin.astype(jnp.float32) * ends[:, :, None]).astype(jnp.bfloat16))
        local = jnp.einsum('shp,sn->hpn', written.astype(jnp.float32), bmat.astype(jnp.float32))
        through = jnp.exp(cum[-1]) * cont[-1]
        state = through[:, None, None] * state + local
        return ((state, ids[-1]), result)
    start = (jnp.zeros((H, P_SIZE, N), jnp.float32), jnp.array(-1, jnp.int32))
    final, results = lax.scan(block_step, start, pieces)
    return results.reshape(JOINED_ITEMS, H * P_SIZE)
```

```python
import functools

import jax
import jax.numpy as jnp
from jax import lax
from jax.experimental import pallas as pl
from jax.experimental.pallas import tpu as pltpu
from jax.sharding import PartitionSpec as P

EPS = 1e-05
MESH = pl.DeviceIdType.MESH
F32 = jnp.float32
BF16 = jnp.bfloat16
LANES = 128
TAIL = 16


def dot(a, b):
    return jnp.dot(a, b, preferred_element_type=F32)


def split2(v):
    high = v.astype(BF16)
    return high, (v - high.astype(F32)).astype(BF16)


def split3(v):
    high, _ = split2(v)
    mid, low = split2(v - high.astype(F32))
    return high, mid, low


def silu(v):
    return v / (1.0 + jnp.exp(-v))


def kernel(
    length, groups,
    x, bc, z, step, decay, docs, taps_x, taps_bc, skip, gain,
    out,
    xc, bcc, base, enter_scale, write_scale, local,
    edge_x, edge_bc, edge_docs,
    pair_out, pair_in, chain_out, chain_in, share_out, share_in, own_entered,
    squares_out, squares_in,
    edge_send, edge_recv, pair_send, pair_recv, chain_send, chain_recv,
    share_send, share_recv, squares_send, squares_recv,
):
    rows, cols = x.shape
    heads = step.shape[1]
    size = cols // heads
    states = bc.shape[1] // 2
    slabs = cols // LANES
    half = slabs // 2
    taps = taps_x.shape[0]
    me = lax.axis_index("seq")
    group = lax.axis_index("head")
    odd = me % 2
    partner = me + 1 - 2 * odd
    peers = [(group + d) % groups for d in range(1, groups)]

    barrier = pltpu.get_barrier_semaphore()
    near = (
        (me > 0, me - 1), (me < length - 1, me + 1), (me > 1, me - 2), (me < length - 2, me + 2),
    )

    for present, other in near:
        @pl.when(present)
        def _(other=other):
            pl.semaphore_signal(barrier, inc=1, device_id=(other, group), device_id_type=MESH)
    for peer in peers:
        pl.semaphore_signal(barrier, inc=1, device_id=(me, peer), device_id_type=MESH)

    def remote(src, dst, send, recv, seq, head):
        return pltpu.make_async_remote_copy(
            src_ref=src, dst_ref=dst, send_sem=send, recv_sem=recv,
            device_id=(seq, head), device_id_type=MESH,
        )

    after = length - 1 - me
    callers = groups - 1
    for position in (me, after):
        callers = callers + (position + length - 1) // length + (position + length - 2) // length
    pl.semaphore_wait(barrier, callers)

    edges = [
        remote(x.at[pl.ds(rows - TAIL, TAIL)], edge_x, edge_send.at[0], edge_recv.at[0], me + 1, group),
        remote(bc.at[pl.ds(rows - TAIL, TAIL)], edge_bc, edge_send.at[1], edge_recv.at[1], me + 1, group),
        remote(docs, edge_docs, edge_send.at[2], edge_recv.at[2], me + 1, group),
    ]

    @pl.when(me < length - 1)
    def _():
        for copy in edges:
            copy.start()

    @pl.when(me == 0)
    def _():
        edge_x[...] = jnp.zeros_like(edge_x)
        edge_bc[...] = jnp.zeros_like(edge_bc)
        edge_docs[...] = jnp.full(edge_docs.shape, -1, jnp.int32)

    doc_row = docs[...].astype(F32)
    doc_col = jnp.transpose(jnp.broadcast_to(doc_row, (LANES, rows)))
    same = jnp.concatenate([doc_col] * (rows // LANES), axis=1) == jnp.broadcast_to(doc_row, (rows, rows))
    gap = lax.broadcasted_iota(jnp.int32, (rows, rows), 0) - lax.broadcasted_iota(jnp.int32, (rows, rows), 1)
    lower = jnp.where(gap >= 0, 1.0, 0.0).astype(BF16)
    moves = [jnp.where(same & (gap == k), 1.0, 0.0).astype(BF16) for k in range(1, taps)]

    def conv(raw, weights, shifts, source):
        total = weights[0:1] * raw.astype(F32)
        for k in range(1, taps):
            total = total + weights[k : k + 1] * dot(shifts[k - 1], source)
        return silu(total).astype(BF16)

    cum = sum(dot(lower, part) for part in split3(decay[...]))
    doc_heads = doc_col[:, :heads]
    ends = jnp.where(doc_heads == doc_row[:, rows - 1 :], jnp.exp(cum[rows - 1 :] - cum), 0.0)
    spread = jnp.where(
        lax.broadcasted_iota(jnp.int32, (2 * heads, cols), 0) % heads
        == lax.broadcasted_iota(jnp.int32, (2 * heads, cols), 1) // size,
        1.0, 0.0,
    ).astype(BF16)

    def widen(v):
        return dot(jnp.concatenate(split2(v), axis=1), spread)

    write_scale[...] = widen(step[...] * ends)
    skip_row = widen(jnp.broadcast_to(skip[...], (8, heads)))[0:1]
    minus = jnp.transpose(cum - jnp.log(step[...]))

    bcc[...] = conv(bc[...], taps_bc[...], moves, bc[...])
    wide = 2 * LANES
    for j in range(cols // wide):
        part = pl.ds(j * wide, wide)
        xc[:, part] = conv(x[:, part], taps_x[:, part], moves, x[:, part])

    @pl.when(me > 0)
    def _():
        for copy in edges:
            copy.wait_recv()

    before = edge_docs[...].astype(F32)
    first = jnp.concatenate([before[:, rows - TAIL :], doc_row[:, :TAIL]], axis=1)
    first_gap = (
        lax.broadcasted_iota(jnp.int32, (TAIL, 2 * TAIL), 0)
        + TAIL
        - lax.broadcasted_iota(jnp.int32, (TAIL, 2 * TAIL), 1)
    )
    first_same = doc_col[:TAIL, : 2 * TAIL] == jnp.broadcast_to(first, (TAIL, 2 * TAIL))
    first_moves = [
        jnp.where(first_same & (first_gap == k), 1.0, 0.0).astype(BF16) for k in range(1, taps)
    ]
    head_bc = bc[:TAIL]
    bcc[:TAIL] = conv(head_bc, taps_bc[...], first_moves, jnp.concatenate([edge_bc[...], head_bc], axis=0))
    head_x = x[:TAIL]
    xc[:TAIL] = conv(head_x, taps_x[...], first_moves, jnp.concatenate([edge_x[...], head_x], axis=0))

    enter_scale[...] = widen(jnp.where(doc_heads == before[:, rows - 1 :], jnp.exp(cum), 0.0))
    b_turned = jnp.transpose(bcc[:, :states].astype(F32)).astype(BF16)
    c_rows = bcc[:, states:]

    def slab(k):
        return pl.ds(pl.multiple_of(k * LANES, LANES), LANES)

    def local_state(k):
        written = (xc[:, slab(k)].astype(F32) * write_scale[:, slab(k)]).astype(BF16)
        return dot(b_turned, written)

    pairs, chains, shares = [], [], []
    for c in range(half):
        k = (1 - odd) * half + c
        pair_out[c, :states] = local_state(k).astype(BF16)
        through = jnp.broadcast_to(enter_scale[rows - 8 :, slab(k)][7:8], (TAIL, LANES))
        high, low = split2(through)
        kind = lax.broadcasted_iota(jnp.int32, (TAIL, LANES), 0)
        pair_out[c, states:] = jnp.where(kind < 8, high.astype(F32), low.astype(F32)).astype(BF16)
        pairs.append(remote(pair_out.at[c], pair_in.at[c], pair_send.at[c], pair_recv.at[c], partner, group))
        chains.append(remote(chain_out.at[c], chain_in.at[c], chain_send.at[c], chain_recv.at[c], me + 2, group))
        shares.append(remote(share_out.at[c], share_in.at[c], share_send.at[c], share_recv.at[c], partner, group))
        pairs[c].start()
    for c in range(half):
        local[c] = local_state(odd * half + c)

    @pl.when(me < 2)
    def _():
        chain_in[...] = jnp.zeros_like(chain_in)

    gram = jnp.where(same & (gap >= 0), dot(c_rows, b_turned), 0.0)
    mid = rows // 2
    lane = lax.broadcasted_iota(jnp.int32, (rows, LANES), 1)
    per_slab = LANES // size
    for j in range(slabs):
        part = pl.ds(j * LANES, LANES)
        values = xc[:, part]
        inner = None
        for i in range(per_slab):
            h = j * per_slab + i
            at = cum[:, h : h + 1]
            minus_row = minus[h : h + 1]
            upper = gram[:mid, :mid] * jnp.exp(jnp.minimum(at[:mid] - minus_row[:, :mid], 0.0))
            left = gram[mid:, :mid] * jnp.exp(at[mid:] - minus_row[:, :mid])
            right = gram[mid:, mid:] * jnp.exp(jnp.minimum(at[mid:] - minus_row[:, mid:], 0.0))
            below = jnp.concatenate([left.astype(BF16), right.astype(BF16)], axis=1)
            term = jnp.concatenate([dot(upper.astype(BF16), values[:mid]), dot(below, values)], axis=0)
            inner = term if inner is None else jnp.where(lane < i * size, inner, term)
        gate = silu(z[:, part].astype(F32))
        base[:, part] = (inner + skip_row[:, j * LANES : (j + 1) * LANES] * values.astype(F32)) * gate
        own_through = enter_scale[rows - 8 :, part]
        enter_scale[: rows - 8, part] = enter_scale[: rows - 8, part] * gate[: rows - 8]
        enter_scale[rows - 8 :, part] = own_through * gate[rows - 8 :]

    is_odd = jnp.full((states, LANES), odd, jnp.int32) == 1
    through_row = widen(
        jnp.broadcast_to(
            jnp.where(doc_heads[rows - 1 :] == before[:, rows - 1 :], jnp.exp(cum[rows - 1 :]), 0.0),
            (8, heads),
        )
    )[0:1]
    for c in range(half):
        pairs[c].wait_recv()
        mine = local[c]
        theirs = pair_in[c, :states].astype(F32)
        extra = pair_in[c, states:].astype(F32)
        their_through = jnp.broadcast_to(extra[0:1] + extra[8:9], (states, LANES))
        own_half = [through_row[:, (s * half + c) * LANES : (s * half + c + 1) * LANES] for s in (0, 1)]
        my_through = jnp.where(
            is_odd,
            jnp.broadcast_to(own_half[1], (states, LANES)),
            jnp.broadcast_to(own_half[0], (states, LANES)),
        )
        even_local = jnp.where(is_odd, theirs, mine)
        odd_local = jnp.where(is_odd, mine, theirs)
        even_through = jnp.where(is_odd, their_through, my_through)
        odd_through = jnp.where(is_odd, my_through, their_through)

        @pl.when(me > 1)
        def _(c=c):
            chains[c].wait_recv()

        incoming = chain_in[c].astype(F32)
        between = even_local + even_through * incoming
        chain_out[c] = (odd_local + odd_through * between).astype(BF16)

        @pl.when(me < length - 2)
        def _(c=c):
            chains[c].start()

        share_out[c] = jnp.where(is_odd, incoming, between).astype(BF16)
        shares[c].start()
        own_entered[c] = jnp.where(is_odd, between, incoming).astype(BF16)

    total = jnp.zeros((rows, LANES), F32)

    def finish(k, entered, total):
        gated = base[:, slab(k)] + dot(c_rows, entered) * enter_scale[:, slab(k)]
        base[:, slab(k)] = gated
        return total + gated * gated

    for c in range(half):
        total = finish(odd * half + c, own_entered[c], total)
    for c in range(half):
        shares[c].wait_recv()
        total = finish((1 - odd) * half + c, share_in[c], total)

    squares = jnp.sum(jnp.transpose(total), axis=0, keepdims=True)
    squares_out[...] = jnp.broadcast_to(squares, squares_out.shape)
    sums = [
        remote(squares_out, squares_in.at[d], squares_send.at[d], squares_recv.at[d], me, peer)
        for d, peer in enumerate(peers)
    ]
    for copy in sums:
        copy.start()
    for d, copy in enumerate(sums):
        copy.wait_recv()
        squares = squares + squares_in[d, 0:1]
    scale = jnp.transpose(jnp.broadcast_to(lax.rsqrt(squares / (cols * groups) + EPS), (LANES, rows)))
    for j in range(slabs):
        part = pl.ds(j * LANES, LANES)
        out[:, part] = (base[:, part] * scale * gain[:, part]).astype(BF16)

    for copy in sums + pairs + shares:
        copy.wait_send()

    @pl.when(me < length - 2)
    def _():
        for copy in chains:
            copy.wait_send()

    @pl.when(me < length - 1)
    def _():
        for copy in edges:
            copy.wait_send()


def body(x_raw, bc_raw, gate_z, step_size, log_decay, doc_ids, conv_x, conv_bc, skip, norm_gain):
    rows, cols = x_raw.shape
    states = bc_raw.shape[1] // 2
    length, groups = lax.axis_size("seq"), lax.axis_size("head")
    half = cols // LANES // 2
    dma = pltpu.SemaphoreType.DMA
    block = pltpu.VMEM((half, states, LANES), BF16)
    pair = pltpu.VMEM((half, states + TAIL, LANES), BF16)
    wide = pltpu.VMEM((rows, cols), F32)
    return pl.pallas_call(
        functools.partial(kernel, length, groups),
        out_shape=jax.ShapeDtypeStruct((rows, cols), BF16),
        in_specs=[pl.BlockSpec(memory_space=pltpu.VMEM)] * 10,
        out_specs=pl.BlockSpec(memory_space=pltpu.VMEM),
        scratch_shapes=[
            pltpu.VMEM((rows, cols), BF16),
            pltpu.VMEM((rows, 2 * states), BF16),
            wide, wide, wide,
            pltpu.VMEM((half, states, LANES), F32),
            pltpu.VMEM((TAIL, cols), BF16),
            pltpu.VMEM((TAIL, 2 * states), BF16),
            pltpu.VMEM((1, rows), jnp.int32),
            pair, pair, block, block, block, block, block,
            pltpu.VMEM((8, rows), F32),
            pltpu.VMEM((groups - 1, 8, rows), F32),
            dma((3,)), dma((3,)),
            dma((half,)), dma((half,)), dma((half,)), dma((half,)), dma((half,)), dma((half,)),
            dma((groups - 1,)), dma((groups - 1,)),
        ],
        compiler_params=pltpu.CompilerParams(
            collective_id=0, has_side_effects=True, vmem_limit_bytes=40 * 1024 * 1024
        ),
        cost_estimate=pl.CostEstimate(flops=10**9, bytes_accessed=2 * 10**6, transcendentals=10**6),
    )(
        x_raw, bc_raw, gate_z, step_size, log_decay, doc_ids.reshape(1, rows),
        conv_x, conv_bc, skip.reshape(1, -1), norm_gain.reshape(1, -1),
    )


def solution(mesh):
    return jax.shard_map(
        body,
        mesh=mesh,
        in_specs=(
            P("seq", "head"),
            P("seq", None),
            P("seq", "head"),
            P("seq", "head"),
            P("seq", "head"),
            P("seq"),
            P(None, "head"),
            P(),
            P("head"),
            P("head"),
        ),
        out_specs=P("seq", "head"),
        check_vma=False,
    )
```

```python
import functools

import jax
import jax.numpy as jnp
from jax import lax
from jax.experimental import pallas as pl
from jax.experimental.pallas import tpu as pltpu
from jax.sharding import PartitionSpec as P

EPS = 1e-05
MESH = pl.DeviceIdType.MESH
F32 = jnp.float32
BF16 = jnp.bfloat16
LANES = 128
TAIL = 16


def dot(a, b):
    return jnp.dot(a, b, preferred_element_type=F32)


def split2(v):
    high = v.astype(BF16)
    return high, (v - high.astype(F32)).astype(BF16)


def split3(v):
    high, _ = split2(v)
    mid, low = split2(v - high.astype(F32))
    return high, mid, low


def silu(v):
    return v / (1.0 + jnp.exp(-v))


def kernel(
    length, groups, rounds,
    x_far, bc_far, z_far, step, decay, docs, taps_x, taps_bc, skip, gain,
    out,
    x, bc, z, load_sem,
    xc, bcc, base, enter_scale, write_scale, local, pair_local,
    edge_x, edge_bc, edge_docs,
    pair_out, pair_in, chain_out, chain_in, share_out, share_in, own_entered,
    squares_out, squares_in,
    edge_send, edge_recv, pair_send, pair_recv, chain_send, chain_recv,
    share_send, share_recv, squares_send, squares_recv,
):
    rows, cols = x.shape
    heads = step.shape[0]
    size = cols // heads
    states = bc.shape[1] // 2
    slabs = cols // LANES
    half = slabs // 2
    taps = taps_x.shape[0]
    me = lax.axis_index("seq")
    group = lax.axis_index("head")
    odd = me % 2
    partner = me + 1 - 2 * odd
    peers = [(group + d) % groups for d in range(1, groups)]

    loads = [
        pltpu.make_async_copy(far, here, load_sem.at[i])
        for i, (far, here) in enumerate(((bc_far, bc), (x_far, x), (z_far, z)))
    ]
    for copy in loads:
        copy.start()

    barrier = pltpu.get_barrier_semaphore()
    near = (
        (me > 0, me - 1), (me < length - 1, me + 1), (me > 1, me - 2), (me < length - 2, me + 2),
    )

    for present, other in near:
        @pl.when(present)
        def _(other=other):
            pl.semaphore_signal(barrier, inc=1, device_id=(other, group), device_id_type=MESH)
    for peer in peers:
        pl.semaphore_signal(barrier, inc=1, device_id=(me, peer), device_id_type=MESH)

    def remote(src, dst, send, recv, seq, head):
        return pltpu.make_async_remote_copy(
            src_ref=src, dst_ref=dst, send_sem=send, recv_sem=recv,
            device_id=(seq, head), device_id_type=MESH,
        )

    after = length - 1 - me
    callers = groups - 1
    for position in (me, after):
        callers = callers + (position + length - 1) // length + (position + length - 2) // length
    pl.semaphore_wait(barrier, callers)

    edges = [
        remote(x_far.at[pl.ds(rows - TAIL, TAIL)], edge_x, edge_send.at[0], edge_recv.at[0], me + 1, group),
        remote(bc_far.at[pl.ds(rows - TAIL, TAIL)], edge_bc, edge_send.at[1], edge_recv.at[1], me + 1, group),
        remote(docs, edge_docs, edge_send.at[2], edge_recv.at[2], me + 1, group),
    ]

    @pl.when(me < length - 1)
    def _():
        for copy in edges:
            copy.start()

    @pl.when(me == 0)
    def _():
        edge_x[...] = jnp.zeros_like(edge_x)
        edge_bc[...] = jnp.zeros_like(edge_bc)
        edge_docs[...] = jnp.full(edge_docs.shape, -1, jnp.int32)

    doc_row = docs[...].astype(F32)
    doc_col = jnp.transpose(jnp.broadcast_to(doc_row, (LANES, rows)))
    same = jnp.concatenate([doc_col] * (rows // LANES), axis=1) == jnp.broadcast_to(doc_row, (rows, rows))
    gap = lax.broadcasted_iota(jnp.int32, (rows, rows), 0) - lax.broadcasted_iota(jnp.int32, (rows, rows), 1)
    upper = jnp.where(gap <= 0, 1.0, 0.0).astype(BF16)
    moves = [jnp.where(same & (gap == k), 1.0, 0.0).astype(BF16) for k in range(1, taps)]

    def conv(raw, weights, shifts, source):
        total = weights[0:1] * raw.astype(F32)
        for k in range(1, taps):
            total = total + weights[k : k + 1] * dot(shifts[k - 1], source)
        return silu(total).astype(BF16)

    parts = dot(jnp.concatenate(split3(decay[...]), axis=0), upper)
    cum_rows = parts[:heads] + parts[heads : 2 * heads] + parts[2 * heads :]
    cum_last = cum_rows[:, rows - 1 :]
    ends = jnp.where(doc_row == doc_row[:, rows - 1 :], jnp.exp(cum_last - cum_rows), 0.0)
    minus = cum_rows - jnp.log(step[...])
    spread = jnp.where(
        lax.broadcasted_iota(jnp.int32, (2 * heads, cols), 0) % heads
        == lax.broadcasted_iota(jnp.int32, (2 * heads, cols), 1) // size,
        1.0, 0.0,
    ).astype(BF16)

    def halves(v):
        return [part.astype(F32) for part in split2(v)]

    turned = jnp.transpose(jnp.concatenate(halves(step[...] * ends) + [cum_rows], axis=0))
    cum = turned[:, 2 * heads :]
    write_scale[...] = dot(turned[:, : 2 * heads].astype(BF16), spread)

    def slab(k):
        return pl.ds(pl.multiple_of(k * LANES, LANES), LANES)

    wide = 2 * LANES

    def main_conv(side):
        for j in range(half // 2):
            part = pl.ds(pl.multiple_of(side * half * LANES + j * wide, wide), wide)
            xc[:, part] = conv(x[:, part], taps_x[:, part], moves, x[:, part])

    def first_conv(side):
        part = pl.ds(pl.multiple_of(side * half * LANES, half * LANES), half * LANES)
        head_x = x[:TAIL, part]
        xc[:TAIL, part] = conv(
            head_x, taps_x[:, part], first_moves, jnp.concatenate([edge_x[:, part], head_x], axis=0)
        )

    loads[0].wait()
    bcc[...] = conv(bc[...], taps_bc[...], moves, bc[...])
    loads[1].wait()
    main_conv(1 - odd)

    @pl.when(me > 0)
    def _():
        for copy in edges:
            copy.wait_recv()

    before = edge_docs[...].astype(F32)
    first = jnp.concatenate([before[:, rows - TAIL :], doc_row[:, :TAIL]], axis=1)
    first_gap = (
        lax.broadcasted_iota(jnp.int32, (TAIL, 2 * TAIL), 0)
        + TAIL
        - lax.broadcasted_iota(jnp.int32, (TAIL, 2 * TAIL), 1)
    )
    first_same = doc_col[:TAIL, : 2 * TAIL] == jnp.broadcast_to(first, (TAIL, 2 * TAIL))
    first_moves = [
        jnp.where(first_same & (first_gap == k), 1.0, 0.0).astype(BF16) for k in range(1, taps)
    ]
    head_bc = bc[:TAIL]
    bcc[:TAIL] = conv(head_bc, taps_bc[...], first_moves, jnp.concatenate([edge_bc[...], head_bc], axis=0))
    first_conv(1 - odd)
    b_turned = jnp.transpose(bcc[:, :states].astype(F32)).astype(BF16)
    c_rows = bcc[:, states:]

    entry_rows = jnp.where(doc_row == before[:, rows - 1 :], jnp.exp(cum_rows), 0.0)
    entry = jnp.transpose(jnp.concatenate(halves(entry_rows), axis=0)).astype(BF16)
    through_row = dot(entry[rows - TAIL :], spread)[TAIL - 1 :]
    low_row = lax.broadcasted_iota(jnp.int32, (TAIL, LANES), 0) >= 8

    def pick(c, side):
        at = [through_row[:, (s * half + c) * LANES : (s * half + c + 1) * LANES] for s in (0, 1)]
        return jnp.where(jnp.full((1, LANES), side, jnp.int32) == 1, at[1], at[0])

    def local_state(k):
        written = (xc[:, slab(k)].astype(F32) * write_scale[:, slab(k)]).astype(BF16)
        return dot(b_turned, written)

    pairs, shares = [], []
    chains = [[] for _ in range(rounds)]
    for c in range(half):
        pair_out[c, :states] = local_state((1 - odd) * half + c).astype(BF16)
        high, low = halves(jnp.broadcast_to(pick(c, 1 - odd), (TAIL, LANES)))
        pair_out[c, states:] = jnp.where(low_row, low, high).astype(BF16)
        pairs.append(remote(pair_out.at[c], pair_in.at[c], pair_send.at[c], pair_recv.at[c], partner, group))
        shares.append(remote(share_out.at[c], share_in.at[c], share_send.at[c], share_recv.at[c], partner, group))
        for r in range(rounds):
            chains[r].append(
                remote(
                    chain_out.at[r, c], chain_in.at[r, c], chain_send.at[r * half + c],
                    chain_recv.at[r * half + c], me + 2, group,
                )
            )
        pairs[c].start()

    @pl.when(me < 2)
    def _():
        chain_in[...] = jnp.zeros_like(chain_in)

    main_conv(odd)
    first_conv(odd)
    for c in range(half):
        local[c] = local_state(odd * half + c)

    enter_scale[...] = dot(entry, spread)
    skip_row = dot(
        jnp.concatenate(split2(jnp.broadcast_to(skip[...], (TAIL, heads))), axis=1), spread
    )[0:1]
    gram = jnp.where(same & (gap >= 0), dot(c_rows, b_turned), 0.0)
    mid = rows // 2
    lane = lax.broadcasted_iota(jnp.int32, (rows, LANES), 1)
    per_slab = LANES // size
    loads[2].wait()

    def inner_slab(j):
        part = pl.ds(j * LANES, LANES)
        values = xc[:, part]
        inner = None
        for i in range(per_slab):
            h = j * per_slab + i
            at = cum[:, h : h + 1]
            minus_row = minus[h : h + 1]
            top = gram[:mid, :mid] * jnp.exp(jnp.minimum(at[:mid] - minus_row[:, :mid], 0.0))
            left = gram[mid:, :mid] * jnp.exp(at[mid:] - minus_row[:, :mid])
            right = gram[mid:, mid:] * jnp.exp(jnp.minimum(at[mid:] - minus_row[:, mid:], 0.0))
            below = jnp.concatenate([left.astype(BF16), right.astype(BF16)], axis=1)
            term = jnp.concatenate([dot(top.astype(BF16), values[:mid]), dot(below, values)], axis=0)
            inner = term if inner is None else jnp.where(lane < i * size, inner, term)
        gate = silu(z[:, part].astype(F32))
        base[:, part] = (inner + skip_row[:, j * LANES : (j + 1) * LANES] * values.astype(F32)) * gate
        enter_scale[:, part] = enter_scale[:, part] * gate

    waiting = list(range(slabs))

    def some_inner(count):
        for _ in range(min(count, len(waiting))):
            inner_slab(waiting.pop(0))

    is_odd = jnp.full((states, LANES), odd, jnp.int32) == 1
    some_inner(slabs // 4)
    through = []
    for c in range(half):
        pairs[c].wait_recv()
        mine = local[c]
        theirs = pair_in[c, :states].astype(F32)
        extra = pair_in[c, states:].astype(F32)
        row_odd = is_odd[:1]
        their_through, my_through = extra[0:1] + extra[8:9], pick(c, odd)
        even_through = jnp.where(row_odd, their_through, my_through)
        odd_through = jnp.where(row_odd, my_through, their_through)
        even_local = jnp.where(is_odd, theirs, mine)
        both = jnp.where(is_odd, mine, theirs) + odd_through * even_local
        chain_out[0, c] = both.astype(BF16)

        @pl.when(me < length - 2)
        def _(c=c):
            chains[0][c].start()

        local[c] = even_local
        pair_local[c] = both
        through.append((even_through, even_through * odd_through))
        some_inner(1)

    for r in range(1, rounds):
        for c in range(half):
            @pl.when(me > 1)
            def _(r=r, c=c):
                chains[r - 1][c].wait_recv()

            chain_out[r, c] = (pair_local[c] + through[c][1] * chain_in[r - 1, c].astype(F32)).astype(BF16)

            @pl.when(me < length - 2)
            def _(r=r, c=c):
                chains[r][c].start()

            if c % 2 == 1:
                some_inner(1)
    some_inner(slabs)

    total = jnp.zeros((rows, LANES), F32)

    def finish(k, entered, total):
        gated = base[:, slab(k)] + dot(c_rows, entered) * enter_scale[:, slab(k)]
        base[:, slab(k)] = gated
        return total + gated * gated

    for c in range(half):
        @pl.when(me > 1)
        def _(c=c):
            chains[rounds - 1][c].wait_recv()

        incoming = chain_in[rounds - 1, c].astype(F32)
        between = local[c] + through[c][0] * incoming
        share_out[c] = jnp.where(is_odd, incoming, between).astype(BF16)
        shares[c].start()
        own_entered[c] = jnp.where(is_odd, between, incoming).astype(BF16)

    for c in range(half):
        total = finish(odd * half + c, own_entered[c], total)
    for c in range(half):
        shares[c].wait_recv()
        total = finish((1 - odd) * half + c, share_in[c], total)

    squares = jnp.sum(jnp.transpose(total), axis=0, keepdims=True)
    squares_out[...] = jnp.broadcast_to(squares, squares_out.shape)
    sums = [
        remote(squares_out, squares_in.at[d], squares_send.at[d], squares_recv.at[d], me, peer)
        for d, peer in enumerate(peers)
    ]
    for copy in sums:
        copy.start()
    for d, copy in enumerate(sums):
        copy.wait_recv()
        squares = squares + squares_in[d, 0:1]
    scale = jnp.transpose(jnp.broadcast_to(lax.rsqrt(squares / (cols * groups) + EPS), (LANES, rows)))
    for j in range(slabs):
        part = pl.ds(j * LANES, LANES)
        out[:, part] = (base[:, part] * scale * gain[:, part]).astype(BF16)

    for copy in sums + pairs + shares:
        copy.wait_send()

    @pl.when(me < length - 2)
    def _():
        for copies in chains:
            for copy in copies:
                copy.wait_send()

    @pl.when(me < length - 1)
    def _():
        for copy in edges:
            copy.wait_send()


def body(x_raw, bc_raw, gate_z, step_size, log_decay, doc_ids, conv_x, conv_bc, skip, norm_gain):
    rows, cols = x_raw.shape
    states = bc_raw.shape[1] // 2
    length, groups = lax.axis_size("seq"), lax.axis_size("head")
    half = cols // LANES // 2
    reach = min(length - 1, min(16 * rows, rows * length // 2) // rows)
    rounds = (reach + 1) // 2
    dma = pltpu.SemaphoreType.DMA
    block = pltpu.VMEM((half, states, LANES), BF16)
    pair = pltpu.VMEM((half, states + TAIL, LANES), BF16)
    chain = pltpu.VMEM((rounds, half, states, LANES), BF16)
    local = pltpu.VMEM((half, states, LANES), F32)
    wide = pltpu.VMEM((rows, cols), F32)
    far = pl.BlockSpec(memory_space=pltpu.HBM)
    return pl.pallas_call(
        functools.partial(kernel, length, groups, rounds),
        out_shape=jax.ShapeDtypeStruct((rows, cols), BF16),
        in_specs=[far] * 3 + [pl.BlockSpec(memory_space=pltpu.VMEM)] * 7,
        out_specs=pl.BlockSpec(memory_space=pltpu.VMEM),
        scratch_shapes=[
            pltpu.VMEM((rows, cols), BF16),
            pltpu.VMEM((rows, 2 * states), BF16),
            pltpu.VMEM((rows, cols), BF16),
            dma((3,)),
            pltpu.VMEM((rows, cols), BF16),
            pltpu.VMEM((rows, 2 * states), BF16),
            wide, wide, wide, local, local,
            pltpu.VMEM((TAIL, cols), BF16),
            pltpu.VMEM((TAIL, 2 * states), BF16),
            pltpu.VMEM((1, rows), jnp.int32),
            pair, pair, chain, chain, block, block, block,
            pltpu.VMEM((8, rows), F32),
            pltpu.VMEM((groups - 1, 8, rows), F32),
            dma((3,)), dma((3,)),
            dma((half,)), dma((half,)), dma((rounds * half,)), dma((rounds * half,)), dma((half,)), dma((half,)),
            dma((groups - 1,)), dma((groups - 1,)),
        ],
        compiler_params=pltpu.CompilerParams(
            collective_id=0, has_side_effects=True, vmem_limit_bytes=40 * 1024 * 1024
        ),
        cost_estimate=pl.CostEstimate(flops=10**9, bytes_accessed=2 * 10**6, transcendentals=10**6),
    )(
        x_raw, bc_raw, gate_z, step_size.T, log_decay.T, doc_ids.reshape(1, rows),
        conv_x, conv_bc, skip.reshape(1, -1), norm_gain.reshape(1, -1),
    )


def solution(mesh):
    return jax.shard_map(
        body,
        mesh=mesh,
        in_specs=(
            P("seq", "head"),
            P("seq", None),
            P("seq", "head"),
            P("seq", "head"),
            P("seq", "head"),
            P("seq"),
            P(None, "head"),
            P(),
            P("head"),
            P("head"),
        ),
        out_specs=P("seq", "head"),
        check_vma=False,
    )
```

```python
import functools

import jax
import jax.numpy as jnp
from jax import lax
from jax.experimental import pallas as pl
from jax.experimental.pallas import tpu as pltpu
from jax.sharding import PartitionSpec as P

EPS = 1e-05
MESH = pl.DeviceIdType.MESH
F32 = jnp.float32
BF16 = jnp.bfloat16
LANES = 128
TAIL = 16


def dot(a, b):
    return jnp.dot(a, b, preferred_element_type=F32)


def split2(v):
    high = v.astype(BF16)
    return high, (v - high.astype(F32)).astype(BF16)


def split3(v):
    high, _ = split2(v)
    mid, low = split2(v - high.astype(F32))
    return high, mid, low


def silu(v):
    return v / (1.0 + jnp.exp(-v))


def kernel(
    length, groups, rounds,
    x_far, bc_far, z_far, step, decay, docs, taps_x, taps_bc, skip, gain,
    out,
    x, bc, z, load_sem,
    xc, bcc, base, enter_scale, write_scale, local, pair_local,
    edge_x, edge_bc, edge_docs,
    pair_out, pair_in, chain_out, chain_in, share_out, share_in, own_entered,
    squares_out, squares_in,
    edge_send, edge_recv, pair_send, pair_recv, chain_send, chain_recv,
    share_send, share_recv, squares_send, squares_recv,
):
    rows, cols = x.shape
    heads = step.shape[0]
    size = cols // heads
    states = bc.shape[1] // 2
    slabs = cols // LANES
    half = slabs // 2
    taps = taps_x.shape[0]
    me = lax.axis_index("seq")
    group = lax.axis_index("head")
    odd = me % 2
    partner = me + 1 - 2 * odd
    peers = [(group + d) % groups for d in range(1, groups)]

    loads = [
        pltpu.make_async_copy(far, here, load_sem.at[i])
        for i, (far, here) in enumerate(((bc_far, bc), (x_far, x), (z_far, z)))
    ]
    for copy in loads:
        copy.start()

    barrier = pltpu.get_barrier_semaphore()
    near = (
        (me > 0, me - 1), (me < length - 1, me + 1), (me > 1, me - 2), (me < length - 2, me + 2),
    )

    for present, other in near:
        @pl.when(present)
        def _(other=other):
            pl.semaphore_signal(barrier, inc=1, device_id=(other, group), device_id_type=MESH)
    for peer in peers:
        pl.semaphore_signal(barrier, inc=1, device_id=(me, peer), device_id_type=MESH)

    def remote(src, dst, send, recv, seq, head):
        return pltpu.make_async_remote_copy(
            src_ref=src, dst_ref=dst, send_sem=send, recv_sem=recv,
            device_id=(seq, head), device_id_type=MESH,
        )

    after = length - 1 - me
    callers = groups - 1
    for position in (me, after):
        callers = callers + (position + length - 1) // length + (position + length - 2) // length
    pl.semaphore_wait(barrier, callers)

    edges = [
        remote(x_far.at[pl.ds(rows - TAIL, TAIL)], edge_x, edge_send.at[0], edge_recv.at[0], me + 1, group),
        remote(bc_far.at[pl.ds(rows - TAIL, TAIL)], edge_bc, edge_send.at[1], edge_recv.at[1], me + 1, group),
        remote(docs, edge_docs, edge_send.at[2], edge_recv.at[2], me + 1, group),
    ]

    @pl.when(me < length - 1)
    def _():
        for copy in edges:
            copy.start()

    @pl.when(me == 0)
    def _():
        edge_x[...] = jnp.zeros_like(edge_x)
        edge_bc[...] = jnp.zeros_like(edge_bc)
        edge_docs[...] = jnp.full(edge_docs.shape, -1, jnp.int32)

    doc_row = docs[...].astype(F32)
    doc_col = jnp.transpose(jnp.broadcast_to(doc_row, (LANES, rows)))
    same = jnp.concatenate([doc_col] * (rows // LANES), axis=1) == jnp.broadcast_to(doc_row, (rows, rows))
    gap = lax.broadcasted_iota(jnp.int32, (rows, rows), 0) - lax.broadcasted_iota(jnp.int32, (rows, rows), 1)
    upper = jnp.where(gap <= 0, 1.0, 0.0).astype(BF16)
    moves = [jnp.where(same & (gap == k), 1.0, 0.0).astype(BF16) for k in range(1, taps)]

    def conv(raw, weights, shifts, source):
        total = weights[0:1] * raw.astype(F32)
        for k in range(1, taps):
            total = total + weights[k : k + 1] * dot(shifts[k - 1], source)
        return silu(total).astype(BF16)

    parts = dot(jnp.concatenate(split3(decay[...]), axis=0), upper)
    cum_rows = parts[:heads] + parts[heads : 2 * heads] + parts[2 * heads :]
    cum_last = cum_rows[:, rows - 1 :]
    ends = jnp.where(doc_row == doc_row[:, rows - 1 :], jnp.exp(cum_last - cum_rows), 0.0)
    minus = cum_rows - jnp.log(step[...])
    spread = jnp.where(
        lax.broadcasted_iota(jnp.int32, (2 * heads, cols), 0) % heads
        == lax.broadcasted_iota(jnp.int32, (2 * heads, cols), 1) // size,
        1.0, 0.0,
    ).astype(BF16)

    def halves(v):
        return [part.astype(F32) for part in split2(v)]

    turned = jnp.transpose(jnp.concatenate(halves(step[...] * ends) + [cum_rows], axis=0))
    cum = turned[:, 2 * heads :]
    write_scale[...] = dot(turned[:, : 2 * heads].astype(BF16), spread)

    def slab(k):
        return pl.ds(pl.multiple_of(k * LANES, LANES), LANES)

    wide = 2 * LANES

    def main_conv(side):
        for j in range(half // 2):
            part = pl.ds(pl.multiple_of(side * half * LANES + j * wide, wide), wide)
            xc[:, part] = conv(x[:, part], taps_x[:, part], moves, x[:, part])

    def first_conv(side):
        part = pl.ds(pl.multiple_of(side * half * LANES, half * LANES), half * LANES)
        head_x = x[:TAIL, part]
        xc[:TAIL, part] = conv(
            head_x, taps_x[:, part], first_moves, jnp.concatenate([edge_x[:, part], head_x], axis=0)
        )

    loads[0].wait()
    bcc[...] = conv(bc[...], taps_bc[...], moves, bc[...])
    loads[1].wait()
    main_conv(1 - odd)

    @pl.when(me > 0)
    def _():
        for copy in edges:
            copy.wait_recv()

    before = edge_docs[...].astype(F32)
    first = jnp.concatenate([before[:, rows - TAIL :], doc_row[:, :TAIL]], axis=1)
    first_gap = (
        lax.broadcasted_iota(jnp.int32, (TAIL, 2 * TAIL), 0)
        + TAIL
        - lax.broadcasted_iota(jnp.int32, (TAIL, 2 * TAIL), 1)
    )
    first_same = doc_col[:TAIL, : 2 * TAIL] == jnp.broadcast_to(first, (TAIL, 2 * TAIL))
    first_moves = [
        jnp.where(first_same & (first_gap == k), 1.0, 0.0).astype(BF16) for k in range(1, taps)
    ]
    head_bc = bc[:TAIL]
    bcc[:TAIL] = conv(head_bc, taps_bc[...], first_moves, jnp.concatenate([edge_bc[...], head_bc], axis=0))
    first_conv(1 - odd)
    b_turned = jnp.transpose(bcc[:, :states].astype(F32)).astype(BF16)
    c_rows = bcc[:, states:]

    entry_rows = jnp.where(doc_row == before[:, rows - 1 :], jnp.exp(cum_rows), 0.0)
    entry = jnp.transpose(jnp.concatenate(halves(entry_rows), axis=0)).astype(BF16)
    through_row = dot(entry[rows - TAIL :], spread)[TAIL - 1 :]
    low_row = lax.broadcasted_iota(jnp.int32, (TAIL, LANES), 0) >= 8

    def pick(c, side):
        at = [through_row[:, (s * half + c) * LANES : (s * half + c + 1) * LANES] for s in (0, 1)]
        return jnp.where(jnp.full((1, LANES), side, jnp.int32) == 1, at[1], at[0])

    def local_state(k):
        written = (xc[:, slab(k)].astype(F32) * write_scale[:, slab(k)]).astype(BF16)
        return dot(b_turned, written)

    pairs, shares = [], []
    chains = [[] for _ in range(rounds)]
    for c in range(half):
        pair_out[c, :states] = local_state((1 - odd) * half + c).astype(BF16)
        high, low = halves(jnp.broadcast_to(pick(c, 1 - odd), (TAIL, LANES)))
        pair_out[c, states:] = jnp.where(low_row, low, high).astype(BF16)
        pairs.append(remote(pair_out.at[c], pair_in.at[c], pair_send.at[c], pair_recv.at[c], partner, group))
        shares.append(remote(share_out.at[c], share_in.at[c], share_send.at[c], share_recv.at[c], partner, group))
        for r in range(rounds):
            chains[r].append(
                remote(
                    chain_out.at[r, c], chain_in.at[r, c], chain_send.at[r * half + c],
                    chain_recv.at[r * half + c], me + 2, group,
                )
            )
        pairs[c].start()

    @pl.when(me < 2)
    def _():
        chain_in[...] = jnp.zeros_like(chain_in)

    main_conv(odd)
    first_conv(odd)
    for c in range(half):
        local[c] = local_state(odd * half + c)

    enter_scale[...] = dot(entry, spread)
    skip_row = dot(
        jnp.concatenate(split2(jnp.broadcast_to(skip[...], (TAIL, heads))), axis=1), spread
    )[0:1]
    gram = jnp.where(same & (gap >= 0), dot(c_rows, b_turned), 0.0)
    mid = rows // 2
    lane = lax.broadcasted_iota(jnp.int32, (rows, LANES), 1)
    per_slab = LANES // size
    loads[2].wait()

    def inner_slab(j):
        part = pl.ds(j * LANES, LANES)
        values = xc[:, part]
        inner = None
        for i in range(per_slab):
            h = j * per_slab + i
            at = cum[:, h : h + 1]
            minus_row = minus[h : h + 1]
            top = gram[:mid, :mid] * jnp.exp(jnp.minimum(at[:mid] - minus_row[:, :mid], 0.0))
            left = gram[mid:, :mid] * jnp.exp(at[mid:] - minus_row[:, :mid])
            right = gram[mid:, mid:] * jnp.exp(jnp.minimum(at[mid:] - minus_row[:, mid:], 0.0))
            below = jnp.concatenate([left.astype(BF16), right.astype(BF16)], axis=1)
            term = jnp.concatenate([dot(top.astype(BF16), values[:mid]), dot(below, values)], axis=0)
            inner = term if inner is None else jnp.where(lane < i * size, inner, term)
        gate = silu(z[:, part].astype(F32))
        base[:, part] = (inner + skip_row[:, j * LANES : (j + 1) * LANES] * values.astype(F32)) * gate
        enter_scale[:, part] = enter_scale[:, part] * gate

    waiting = list(range(slabs))

    def some_inner(count):
        for _ in range(min(count, len(waiting))):
            inner_slab(waiting.pop(0))

    is_odd = jnp.full((states, LANES), odd, jnp.int32) == 1
    some_inner(slabs // 4)
    through = []
    for c in range(half):
        pairs[c].wait_recv()
        mine = local[c]
        theirs = pair_in[c, :states].astype(F32)
        extra = pair_in[c, states:].astype(F32)
        row_odd = is_odd[:1]
        their_through, my_through = extra[0:1] + extra[8:9], pick(c, odd)
        even_through = jnp.where(row_odd, their_through, my_through)
        odd_through = jnp.where(row_odd, my_through, their_through)
        even_local = jnp.where(is_odd, theirs, mine)
        both = jnp.where(is_odd, mine, theirs) + odd_through * even_local
        chain_out[0, c] = both.astype(BF16)

        @pl.when(me < length - 2)
        def _(c=c):
            chains[0][c].start()

        local[c] = even_local
        pair_local[c] = both
        through.append((even_through, even_through * odd_through))
        some_inner(1)

    for r in range(1, rounds):
        for c in range(half):
            @pl.when(me > 1)
            def _(r=r, c=c):
                chains[r - 1][c].wait_recv()

            chain_out[r, c] = (pair_local[c] + through[c][1] * chain_in[r - 1, c].astype(F32)).astype(BF16)

            @pl.when(me < length - 2)
            def _(r=r, c=c):
                chains[r][c].start()

            if c % 2 == 1:
                some_inner(1)
    some_inner(slabs)

    total = jnp.zeros((rows, LANES), F32)

    def finish(k, entered, total):
        gated = base[:, slab(k)] + dot(c_rows, entered) * enter_scale[:, slab(k)]
        base[:, slab(k)] = gated
        return total + gated * gated

    for c in range(half):
        @pl.when(me > 1)
        def _(c=c):
            chains[rounds - 1][c].wait_recv()

        incoming = chain_in[rounds - 1, c].astype(F32)
        between = local[c] + through[c][0] * incoming
        share_out[c] = jnp.where(is_odd, incoming, between).astype(BF16)
        shares[c].start()
        own_entered[c] = jnp.where(is_odd, between, incoming).astype(BF16)

    for c in range(half):
        total = finish(odd * half + c, own_entered[c], total)
    for c in range(half):
        shares[c].wait_recv()
        total = finish((1 - odd) * half + c, share_in[c], total)

    squares = jnp.sum(jnp.transpose(total), axis=0, keepdims=True)
    squares_out[...] = jnp.broadcast_to(squares, squares_out.shape)
    sums = [
        remote(squares_out, squares_in.at[d], squares_send.at[d], squares_recv.at[d], me, peer)
        for d, peer in enumerate(peers)
    ]
    for copy in sums:
        copy.start()
    for d, copy in enumerate(sums):
        copy.wait_recv()
        squares = squares + squares_in[d, 0:1]
    scale = jnp.transpose(jnp.broadcast_to(lax.rsqrt(squares / (cols * groups) + EPS), (LANES, rows)))
    for j in range(slabs):
        part = pl.ds(j * LANES, LANES)
        out[:, part] = (base[:, part] * scale * gain[:, part]).astype(BF16)

    for copy in sums + pairs + shares:
        copy.wait_send()

    @pl.when(me < length - 2)
    def _():
        for copies in chains:
            for copy in copies:
                copy.wait_send()

    @pl.when(me < length - 1)
    def _():
        for copy in edges:
            copy.wait_send()


def body(x_raw, bc_raw, gate_z, step_size, log_decay, doc_ids, conv_x, conv_bc, skip, norm_gain):
    rows, cols = x_raw.shape
    states = bc_raw.shape[1] // 2
    length, groups = lax.axis_size("seq"), lax.axis_size("head")
    half = cols // LANES // 2
    reach = min(length - 1, min(16 * rows, rows * length // 2) // rows)
    rounds = (reach + 1) // 2
    dma = pltpu.SemaphoreType.DMA
    block = pltpu.VMEM((half, states, LANES), BF16)
    pair = pltpu.VMEM((half, states + TAIL, LANES), BF16)
    chain = pltpu.VMEM((rounds, half, states, LANES), BF16)
    local = pltpu.VMEM((half, states, LANES), F32)
    wide = pltpu.VMEM((rows, cols), F32)
    far = pl.BlockSpec(memory_space=pltpu.HBM)
    return pl.pallas_call(
        functools.partial(kernel, length, groups, rounds),
        out_shape=jax.ShapeDtypeStruct((rows, cols), BF16),
        in_specs=[far] * 3 + [pl.BlockSpec(memory_space=pltpu.VMEM)] * 7,
        out_specs=pl.BlockSpec(memory_space=pltpu.VMEM),
        scratch_shapes=[
            pltpu.VMEM((rows, cols), BF16),
            pltpu.VMEM((rows, 2 * states), BF16),
            pltpu.VMEM((rows, cols), BF16),
            dma((3,)),
            pltpu.VMEM((rows, cols), BF16),
            pltpu.VMEM((rows, 2 * states), BF16),
            wide, wide, wide, local, local,
            pltpu.VMEM((TAIL, cols), BF16),
            pltpu.VMEM((TAIL, 2 * states), BF16),
            pltpu.VMEM((1, rows), jnp.int32),
            pair, pair, chain, chain, block, block, block,
            pltpu.VMEM((8, rows), F32),
            pltpu.VMEM((groups - 1, 8, rows), F32),
            dma((3,)), dma((3,)),
            dma((half,)), dma((half,)), dma((rounds * half,)), dma((rounds * half,)), dma((half,)), dma((half,)),
            dma((groups - 1,)), dma((groups - 1,)),
        ],
        compiler_params=pltpu.CompilerParams(
            collective_id=0, has_side_effects=True, vmem_limit_bytes=62 * 1024 * 1024
        ),
        cost_estimate=pl.CostEstimate(flops=10**9, bytes_accessed=2 * 10**6, transcendentals=10**6),
    )(
        x_raw, bc_raw, gate_z, step_size.T, log_decay.T, doc_ids.reshape(1, rows),
        conv_x, conv_bc, skip.reshape(1, -1), norm_gain.reshape(1, -1),
    )


def solution(mesh):
    return jax.shard_map(
        body,
        mesh=mesh,
        in_specs=(
            P("seq", "head"),
            P("seq", None),
            P("seq", "head"),
            P("seq", "head"),
            P("seq", "head"),
            P("seq"),
            P(None, "head"),
            P(),
            P("head"),
            P("head"),
        ),
        out_specs=P("seq", "head"),
        check_vma=False,
    )
```

```python
import functools

import jax
import jax.numpy as jnp
from jax import lax
from jax.experimental import pallas as pl
from jax.experimental.pallas import tpu as pltpu
from jax.sharding import PartitionSpec as P

EPS = 1e-05
MESH = pl.DeviceIdType.MESH
F32 = jnp.float32
BF16 = jnp.bfloat16
LANES = 128
TAIL = 16


def dot(a, b):
    return jnp.dot(a, b, preferred_element_type=F32)


def split2(v):
    high = v.astype(BF16)
    return high, (v - high.astype(F32)).astype(BF16)


def split3(v):
    high, _ = split2(v)
    mid, low = split2(v - high.astype(F32))
    return high, mid, low


def silu(v):
    return v / (1.0 + jnp.exp(-v))


def kernel(
    length, groups, rounds,
    x_far, bc_far, z_far, step_far, decay_far, docs_far, taps_x_far, taps_bc_far, skip_far, gain_far,
    out_far,
    x, bc, z, step, decay, docs, taps_x, taps_bc, skip, gain, out, load_sem, store_sem,
    xc, bcc, base, enter_scale, write_scale, local, pair_local,
    edge_x, edge_bc, edge_docs,
    pair_out, pair_in, chain_out, chain_in, share_out, share_in, own_entered,
    squares_out, squares_in,
    edge_send, edge_recv, pair_send, pair_recv, chain_send, chain_recv,
    share_send, share_recv, squares_send, squares_recv,
):
    rows, cols = x.shape
    heads = step.shape[0]
    size = cols // heads
    states = bc.shape[1] // 2
    slabs = cols // LANES
    half = slabs // 2
    taps = taps_x.shape[0]
    me = lax.axis_index("seq")
    group = lax.axis_index("head")
    odd = me % 2
    partner = me + 1 - 2 * odd
    peers = [(group + d) % groups for d in range(1, groups)]

    barrier = pltpu.get_barrier_semaphore()
    near = (
        (me > 0, me - 1), (me < length - 1, me + 1), (me > 1, me - 2), (me < length - 2, me + 2),
    )

    for present, other in near:
        @pl.when(present)
        def _(other=other):
            pl.semaphore_signal(barrier, inc=1, device_id=(other, group), device_id_type=MESH)
    for peer in peers:
        pl.semaphore_signal(barrier, inc=1, device_id=(me, peer), device_id_type=MESH)

    order = (
        (docs_far, docs), (decay_far, decay), (step_far, step), (bc_far, bc), (taps_bc_far, taps_bc),
        (x_far, x), (taps_x_far, taps_x), (skip_far, skip), (z_far, z), (gain_far, gain),
    )
    loads = [
        pltpu.make_async_copy(far, here, load_sem.at[i]) for i, (far, here) in enumerate(order)
    ]
    for copy in loads:
        copy.start()

    def remote(src, dst, send, recv, seq, head):
        return pltpu.make_async_remote_copy(
            src_ref=src, dst_ref=dst, send_sem=send, recv_sem=recv,
            device_id=(seq, head), device_id_type=MESH,
        )

    after = length - 1 - me
    callers = groups - 1
    for position in (me, after):
        callers = callers + (position + length - 1) // length + (position + length - 2) // length
    pl.semaphore_wait(barrier, callers)

    edges = [
        remote(x_far.at[pl.ds(rows - TAIL, TAIL)], edge_x, edge_send.at[0], edge_recv.at[0], me + 1, group),
        remote(bc_far.at[pl.ds(rows - TAIL, TAIL)], edge_bc, edge_send.at[1], edge_recv.at[1], me + 1, group),
        remote(docs_far, edge_docs, edge_send.at[2], edge_recv.at[2], me + 1, group),
    ]

    @pl.when(me < length - 1)
    def _():
        for copy in edges:
            copy.start()

    @pl.when(me == 0)
    def _():
        edge_x[...] = jnp.zeros_like(edge_x)
        edge_bc[...] = jnp.zeros_like(edge_bc)
        edge_docs[...] = jnp.full(edge_docs.shape, -1, jnp.int32)

    for copy in loads[:3]:
        copy.wait()
    doc_row = docs[...].astype(F32)
    doc_col = jnp.transpose(jnp.broadcast_to(doc_row, (LANES, rows)))
    same = jnp.concatenate([doc_col] * (rows // LANES), axis=1) == jnp.broadcast_to(doc_row, (rows, rows))
    gap = lax.broadcasted_iota(jnp.int32, (rows, rows), 0) - lax.broadcasted_iota(jnp.int32, (rows, rows), 1)
    upper = jnp.where(gap <= 0, 1.0, 0.0).astype(BF16)
    moves = [jnp.where(same & (gap == k), 1.0, 0.0).astype(BF16) for k in range(1, taps)]

    def conv(raw, weights, shifts, source):
        total = weights[0:1] * raw.astype(F32)
        for k in range(1, taps):
            total = total + weights[k : k + 1] * dot(shifts[k - 1], source)
        return silu(total).astype(BF16)

    parts = dot(jnp.concatenate(split3(decay[...]), axis=0), upper)
    cum_rows = parts[:heads] + parts[heads : 2 * heads] + parts[2 * heads :]
    cum_last = cum_rows[:, rows - 1 :]
    ends = jnp.where(doc_row == doc_row[:, rows - 1 :], jnp.exp(cum_last - cum_rows), 0.0)
    minus = cum_rows - jnp.log(step[...])
    spread = jnp.where(
        lax.broadcasted_iota(jnp.int32, (2 * heads, cols), 0) % heads
        == lax.broadcasted_iota(jnp.int32, (2 * heads, cols), 1) // size,
        1.0, 0.0,
    ).astype(BF16)

    def halves(v):
        return [part.astype(F32) for part in split2(v)]

    turned = jnp.transpose(jnp.concatenate(halves(step[...] * ends) + [cum_rows], axis=0))
    cum = turned[:, 2 * heads :]
    write_scale[...] = dot(turned[:, : 2 * heads].astype(BF16), spread)

    def slab(k):
        return pl.ds(pl.multiple_of(k * LANES, LANES), LANES)

    wide = 2 * LANES

    def main_conv(side):
        for j in range(half // 2):
            part = pl.ds(pl.multiple_of(side * half * LANES + j * wide, wide), wide)
            xc[:, part] = conv(x[:, part], taps_x[:, part], moves, x[:, part])

    def first_conv(side):
        part = pl.ds(pl.multiple_of(side * half * LANES, half * LANES), half * LANES)
        head_x = x[:TAIL, part]
        xc[:TAIL, part] = conv(
            head_x, taps_x[:, part], first_moves, jnp.concatenate([edge_x[:, part], head_x], axis=0)
        )

    for copy in loads[3:5]:
        copy.wait()
    bcc[...] = conv(bc[...], taps_bc[...], moves, bc[...])
    for copy in loads[5:7]:
        copy.wait()
    main_conv(1 - odd)

    @pl.when(me > 0)
    def _():
        for copy in edges:
            copy.wait_recv()

    before = edge_docs[...].astype(F32)
    first = jnp.concatenate([before[:, rows - TAIL :], doc_row[:, :TAIL]], axis=1)
    first_gap = (
        lax.broadcasted_iota(jnp.int32, (TAIL, 2 * TAIL), 0)
        + TAIL
        - lax.broadcasted_iota(jnp.int32, (TAIL, 2 * TAIL), 1)
    )
    first_same = doc_col[:TAIL, : 2 * TAIL] == jnp.broadcast_to(first, (TAIL, 2 * TAIL))
    first_moves = [
        jnp.where(first_same & (first_gap == k), 1.0, 0.0).astype(BF16) for k in range(1, taps)
    ]
    head_bc = bc[:TAIL]
    bcc[:TAIL] = conv(head_bc, taps_bc[...], first_moves, jnp.concatenate([edge_bc[...], head_bc], axis=0))
    first_conv(1 - odd)
    b_turned = jnp.transpose(bcc[:, :states].astype(F32)).astype(BF16)
    c_rows = bcc[:, states:]

    entry_rows = jnp.where(doc_row == before[:, rows - 1 :], jnp.exp(cum_rows), 0.0)
    entry = jnp.transpose(jnp.concatenate(halves(entry_rows), axis=0)).astype(BF16)
    through_row = dot(entry[rows - TAIL :], spread)[TAIL - 1 :]
    low_row = lax.broadcasted_iota(jnp.int32, (TAIL, LANES), 0) >= 8

    def pick(c, side):
        at = [through_row[:, (s * half + c) * LANES : (s * half + c + 1) * LANES] for s in (0, 1)]
        return jnp.where(jnp.full((1, LANES), side, jnp.int32) == 1, at[1], at[0])

    def local_state(k):
        written = (xc[:, slab(k)].astype(F32) * write_scale[:, slab(k)]).astype(BF16)
        return dot(b_turned, written)

    pairs, shares = [], []
    chains = [[] for _ in range(rounds)]
    for c in range(half):
        pair_out[c, :states] = local_state((1 - odd) * half + c).astype(BF16)
        high, low = halves(jnp.broadcast_to(pick(c, 1 - odd), (TAIL, LANES)))
        pair_out[c, states:] = jnp.where(low_row, low, high).astype(BF16)
        pairs.append(remote(pair_out.at[c], pair_in.at[c], pair_send.at[c], pair_recv.at[c], partner, group))
        shares.append(remote(share_out.at[c], share_in.at[c], share_send.at[c], share_recv.at[c], partner, group))
        for r in range(rounds):
            chains[r].append(
                remote(
                    chain_out.at[r, c], chain_in.at[r, c], chain_send.at[r * half + c],
                    chain_recv.at[r * half + c], me + 2, group,
                )
            )
        pairs[c].start()

    @pl.when(me < 2)
    def _():
        chain_in[...] = jnp.zeros_like(chain_in)

    main_conv(odd)
    first_conv(odd)
    for c in range(half):
        local[c] = local_state(odd * half + c)

    enter_scale[...] = dot(entry, spread)
    loads[7].wait()
    skip_row = dot(
        jnp.concatenate(split2(jnp.broadcast_to(skip[...], (TAIL, heads))), axis=1), spread
    )[0:1]
    gram = jnp.where(same & (gap >= 0), dot(c_rows, b_turned), 0.0)
    mid = rows // 2
    lane = lax.broadcasted_iota(jnp.int32, (rows, LANES), 1)
    per_slab = LANES // size
    for copy in loads[8:]:
        copy.wait()

    def inner_slab(j):
        part = pl.ds(j * LANES, LANES)
        values = xc[:, part]
        inner = None
        for i in range(per_slab):
            h = j * per_slab + i
            at = cum[:, h : h + 1]
            minus_row = minus[h : h + 1]
            top = gram[:mid, :mid] * jnp.exp(jnp.minimum(at[:mid] - minus_row[:, :mid], 0.0))
            left = gram[mid:, :mid] * jnp.exp(at[mid:] - minus_row[:, :mid])
            right = gram[mid:, mid:] * jnp.exp(jnp.minimum(at[mid:] - minus_row[:, mid:], 0.0))
            below = jnp.concatenate([left.astype(BF16), right.astype(BF16)], axis=1)
            term = jnp.concatenate([dot(top.astype(BF16), values[:mid]), dot(below, values)], axis=0)
            inner = term if inner is None else jnp.where(lane < i * size, inner, term)
        gate = silu(z[:, part].astype(F32))
        base[:, part] = (inner + skip_row[:, j * LANES : (j + 1) * LANES] * values.astype(F32)) * gate
        enter_scale[:, part] = enter_scale[:, part] * gate

    waiting = list(range(slabs))

    def some_inner(count):
        for _ in range(min(count, len(waiting))):
            inner_slab(waiting.pop(0))

    is_odd = jnp.full((states, LANES), odd, jnp.int32) == 1
    some_inner(slabs // 4)
    through = []
    for c in range(half):
        pairs[c].wait_recv()
        mine = local[c]
        theirs = pair_in[c, :states].astype(F32)
        extra = pair_in[c, states:].astype(F32)
        row_odd = is_odd[:1]
        their_through, my_through = extra[0:1] + extra[8:9], pick(c, odd)
        even_through = jnp.where(row_odd, their_through, my_through)
        odd_through = jnp.where(row_odd, my_through, their_through)
        even_local = jnp.where(is_odd, theirs, mine)
        both = jnp.where(is_odd, mine, theirs) + odd_through * even_local
        chain_out[0, c] = both.astype(BF16)

        @pl.when(me < length - 2)
        def _(c=c):
            chains[0][c].start()

        local[c] = even_local
        pair_local[c] = both
        through.append((even_through, even_through * odd_through))
        some_inner(1)

    for r in range(1, rounds):
        for c in range(half):
            @pl.when(me > 1)
            def _(r=r, c=c):
                chains[r - 1][c].wait_recv()

            chain_out[r, c] = (pair_local[c] + through[c][1] * chain_in[r - 1, c].astype(F32)).astype(BF16)

            @pl.when(me < length - 2)
            def _(r=r, c=c):
                chains[r][c].start()

            if c % 2 == 1:
                some_inner(1)
    some_inner(slabs)

    total = jnp.zeros((rows, LANES), F32)

    def finish(k, entered, total):
        gated = base[:, slab(k)] + dot(c_rows, entered) * enter_scale[:, slab(k)]
        base[:, slab(k)] = gated
        return total + gated * gated

    for c in range(half):
        @pl.when(me > 1)
        def _(c=c):
            chains[rounds - 1][c].wait_recv()

        incoming = chain_in[rounds - 1, c].astype(F32)
        between = local[c] + through[c][0] * incoming
        share_out[c] = jnp.where(is_odd, incoming, between).astype(BF16)
        shares[c].start()
        own_entered[c] = jnp.where(is_odd, between, incoming).astype(BF16)

    for c in range(half):
        total = finish(odd * half + c, own_entered[c], total)
    for c in range(half):
        shares[c].wait_recv()
        total = finish((1 - odd) * half + c, share_in[c], total)

    squares = jnp.sum(jnp.transpose(total), axis=0, keepdims=True)
    squares_out[...] = jnp.broadcast_to(squares, squares_out.shape)
    sums = [
        remote(squares_out, squares_in.at[d], squares_send.at[d], squares_recv.at[d], me, peer)
        for d, peer in enumerate(peers)
    ]
    for copy in sums:
        copy.start()
    for d, copy in enumerate(sums):
        copy.wait_recv()
        squares = squares + squares_in[d, 0:1]
    scale = jnp.transpose(jnp.broadcast_to(lax.rsqrt(squares / (cols * groups) + EPS), (LANES, rows)))
    stores = []
    for j in range(slabs):
        part = pl.ds(j * LANES, LANES)
        out[:, part] = (base[:, part] * scale * gain[:, part]).astype(BF16)
        if j % 2 == 1:
            done = pl.ds((j - 1) * LANES, 2 * LANES)
            stores.append(
                pltpu.make_async_copy(out.at[:, done], out_far.at[:, done], store_sem.at[j // 2])
            )
            stores[-1].start()

    for copy in stores:
        copy.wait()
    for copy in sums + pairs + shares:
        copy.wait_send()

    @pl.when(me < length - 2)
    def _():
        for copies in chains:
            for copy in copies:
                copy.wait_send()

    @pl.when(me < length - 1)
    def _():
        for copy in edges:
            copy.wait_send()


def body(x_raw, bc_raw, gate_z, step_size, log_decay, doc_ids, conv_x, conv_bc, skip, norm_gain):
    rows, cols = x_raw.shape
    states = bc_raw.shape[1] // 2
    length, groups = lax.axis_size("seq"), lax.axis_size("head")
    half = cols // LANES // 2
    reach = min(length - 1, min(16 * rows, rows * length // 2) // rows)
    rounds = (reach + 1) // 2
    dma = pltpu.SemaphoreType.DMA
    block = pltpu.VMEM((half, states, LANES), BF16)
    pair = pltpu.VMEM((half, states + TAIL, LANES), BF16)
    chain = pltpu.VMEM((rounds, half, states, LANES), BF16)
    local = pltpu.VMEM((half, states, LANES), F32)
    wide = pltpu.VMEM((rows, cols), F32)
    steps = pltpu.VMEM((step_size.shape[1], rows), F32)
    far = pl.BlockSpec(memory_space=pltpu.HBM)
    return pl.pallas_call(
        functools.partial(kernel, length, groups, rounds),
        out_shape=jax.ShapeDtypeStruct((rows, cols), BF16),
        in_specs=[far] * 10,
        out_specs=far,
        scratch_shapes=[
            pltpu.VMEM((rows, cols), BF16),
            pltpu.VMEM((rows, 2 * states), BF16),
            pltpu.VMEM((rows, cols), BF16),
            steps, steps,
            pltpu.VMEM((1, rows), jnp.int32),
            pltpu.VMEM(conv_x.shape, F32),
            pltpu.VMEM(conv_bc.shape, F32),
            pltpu.VMEM((1, step_size.shape[1]), F32),
            pltpu.VMEM((1, cols), F32),
            pltpu.VMEM((rows, cols), BF16),
            dma((10,)), dma((half,)),
            pltpu.VMEM((rows, cols), BF16),
            pltpu.VMEM((rows, 2 * states), BF16),
            wide, wide, wide, local, local,
            pltpu.VMEM((TAIL, cols), BF16),
            pltpu.VMEM((TAIL, 2 * states), BF16),
            pltpu.VMEM((1, rows), jnp.int32),
            pair, pair, chain, chain, block, block, block,
            pltpu.VMEM((8, rows), F32),
            pltpu.VMEM((groups - 1, 8, rows), F32),
            dma((3,)), dma((3,)),
            dma((half,)), dma((half,)), dma((rounds * half,)), dma((rounds * half,)), dma((half,)), dma((half,)),
            dma((groups - 1,)), dma((groups - 1,)),
        ],
        compiler_params=pltpu.CompilerParams(
            collective_id=0, has_side_effects=True, vmem_limit_bytes=62 * 1024 * 1024
        ),
        cost_estimate=pl.CostEstimate(flops=10**9, bytes_accessed=2 * 10**6, transcendentals=10**6),
    )(
        x_raw, bc_raw, gate_z, step_size.T, log_decay.T, doc_ids.reshape(1, rows),
        conv_x, conv_bc, skip.reshape(1, -1), norm_gain.reshape(1, -1),
    )


def solution(mesh):
    return jax.shard_map(
        body,
        mesh=mesh,
        in_specs=(
            P("seq", "head"),
            P("seq", None),
            P("seq", "head"),
            P("seq", "head"),
            P("seq", "head"),
            P("seq"),
            P(None, "head"),
            P(),
            P("head"),
            P("head"),
        ),
        out_specs=P("seq", "head"),
        check_vma=False,
    )
```
